32 devices in a mesh: groups: 2 (over y), seq: 8 (over z, x), chan: 1, section: 2 (over core).
Axes of the slice: x: 2, y: 2, z: 4, core: 2. Of those that a mesh axis runs over, the one named last changes fastest.
Arguments:
- queries: bfloat16 [8192, 8192], P(('groups', 'seq', 'section'), 'chan'), parts along dimension 0, may hold values from -6 to 6
- key_proj: bfloat16 [8192, 8192], P(('groups', 'seq', 'section'), 'chan'), parts along dimension 0, may hold values from -6 to 6
- value_proj: bfloat16 [8192, 8192], P(('groups', 'seq', 'section'), 'chan'), parts along dimension 0, may hold values from -6 to 6
- filter_taps: bfloat16 [512, 128], P('chan'), may hold values from -0.5 to 0.5
- skip_gain: float32 [8192], P('chan'), may hold values from -3 to 3
- out_weight: bfloat16 [8192, 4096], P('chan', ('seq', 'section')), may hold values from -0.09375 to 0.09375
- residual: bfloat16 [8192, 4096], P(('groups', 'seq', 'section'), 'chan'), parts along dimension 0, may hold values from -6 to 6
Outputs:
- layer_out: bfloat16 [8192, 4096], P(('groups', 'seq', 'section'), 'chan'), parts along dimension 0
The draws below stay inside these ranges and needn't reach their ends.
There are 2 independent parts, one for each index of `groups`. The reference program is written for one: setup_inputs(seed, part) draws one part's arguments, and reference() takes and returns one part's arrays. A program takes and returns all parts, laid end to end along the dimension named above; an argument that names none is the same for every part. Nothing has to cross between parts.
All inputs are finite; a program needn't handle non-finite values.
Results may differ from the reference program's by a relative error of at most 0.0053.
Values may be sent and summed in bfloat16 or wider, within the bound.
No kernel may reach another device: no remote copies, remote signals or barrier semaphores. Data moves between devices by JAX's collectives and lax.ppermute only.
A program may use at most 256 MiB of HBM per device.

```python
import jax
import jax.numpy as jnp
from jax import lax

C = 8192
OUT = 4096
GROUPS = 512
BLOCK = 128
TOKENS = 4096


def with_spikes(result, stream_key, source, target, blocks, factor):
    def block_of(dim):
        return (jnp.arange(result.shape[dim]) // (result.shape[dim] // blocks)).reshape((-1,) + (1,) * (result.ndim - 1 - dim))

    first = jax.random.permutation(stream_key, blocks)[block_of(target)]
    other_side = (block_of(target) + blocks // 2) % blocks
    return jnp.where((block_of(source) == first) | (block_of(source) == other_side), factor * result, result)


def shard_levels(rng, shape, pieces, smallest, high):
    def one(position, shards_of):
        heights = jax.random.uniform(jax.random.fold_in(jax.random.fold_in(rng, 6), position), (shards_of,), jnp.float32, smallest / len(pieces), high / len(pieces))
        return jnp.repeat(jnp.exp(heights), shape[position] // shards_of).reshape((-1,) + (1,) * (len(shape) - position - 1))

    factor_of = one(*pieces[0])
    for cut in pieces[1:]:
        factor_of = factor_of * one(*cut)
    return factor_of


def gaussian(stream_key, extent, deviation, reach, cuts=(), dtype=jnp.bfloat16):
    result = deviation * jax.random.normal(stream_key, extent, jnp.float32)
    if cuts:
        result = result * shard_levels(stream_key, extent, cuts, -0.22, 0.18)
    return jnp.clip(result, -reach, reach).astype(dtype)


def heavy_noise(rng, dims, deviation, bound, cuts, heavy, dtype=jnp.bfloat16):
    drawn = deviation * jax.random.normal(rng, dims, jnp.float32)
    if cuts:
        drawn = drawn * shard_levels(rng, dims, cuts, -0.22, 0.18)
    return jnp.clip(with_spikes(drawn, jax.random.fold_in(rng, 3), *heavy), -bound, bound).astype(dtype)


def setup_inputs(seed: int = 0, part: int = 0) -> dict:
    splits = jax.random.split(jax.random.key(seed), 8)
    own_keys = jax.random.split(jax.random.fold_in(splits[7], part), 8)
    return {
        "queries": gaussian(own_keys[0], (TOKENS, C), 1.0, 6.0, ((0, 16),)),
        "key_proj": gaussian(own_keys[1], (TOKENS, C), 1.0, 6.0, ((0, 16),)),
        "value_proj": gaussian(own_keys[2], (TOKENS, C), 1.0, 6.0, ((0, 16),)),
        "filter_taps": gaussian(splits[3], (GROUPS, BLOCK), BLOCK ** -0.5, 0.5),
        "skip_gain": gaussian(splits[4], (C,), 0.5, 3.0, (), jnp.float32),
        "out_weight": heavy_noise(splits[5], (C, OUT), C ** -0.5, 0.09375, ((1, 16),), (0, 1, 16, 2.0)),
        "residual": gaussian(own_keys[6], (TOKENS, OUT), 1.0, 6.0, ((0, 16),)),
    }


def reference(queries, key_proj, value_proj, filter_taps, skip_gain, out_weight, residual):
    product = (key_proj.astype(jnp.float32) * value_proj.astype(jnp.float32)).astype(jnp.bfloat16)
    product_f = product.astype(jnp.float32)
    channel_taps = jnp.repeat(filter_taps.astype(jnp.float32), C // GROUPS, axis=0)
    padded = jnp.pad(product_f, ((BLOCK - 1, 0), (0, 0)))

    def add_tap(offset, convolved):
        start = (BLOCK - 1 - jnp.asarray(offset)).astype(jnp.int32)
        shifted = lax.dynamic_slice_in_dim(padded, start, TOKENS, 0)
        column = lax.dynamic_slice_in_dim(channel_taps, jnp.asarray(offset).astype(jnp.int32), 1, 1)[:, 0]
        return convolved + shifted * column[None, :]

    convolved = lax.fori_loop(0, BLOCK, add_tap, jnp.zeros((TOKENS, C), jnp.float32))
    gated = (queries.astype(jnp.float32) * (convolved + skip_gain[None, :] * product_f)).astype(jnp.bfloat16)
    projected = jnp.dot(gated, out_weight, preferred_element_type=jnp.float32)
    return (residual.astype(jnp.float32) + projected).astype(jnp.bfloat16)
```

```python
import functools

import jax
import jax.numpy as jnp
from jax import lax
from jax.experimental import pallas as pl
from jax.experimental.pallas import tpu as pltpu
from jax.sharding import PartitionSpec as P

LANES = 128
SEQ = ("seq", "section")
EVERY = ("groups", "seq", "section")
F32, BF16 = jnp.float32, jnp.bfloat16


def cost(us):
    return pl.CostEstimate(flops=int(us * 1.1e9), bytes_accessed=1, transcendentals=0)


def pass_kernel(*refs):
    pass


def after(values, *waits, weight=0):
    return pl.pallas_call(
        pass_kernel,
        in_specs=[pl.BlockSpec(memory_space=pl.ANY)] * (len(values) + len(waits)),
        out_specs=[pl.BlockSpec(memory_space=pl.ANY)] * len(values),
        out_shape=[jax.ShapeDtypeStruct(v.shape, v.dtype) for v in values],
        input_output_aliases={i: i for i in range(len(values))},
        cost_estimate=cost(weight),
    )(*values, *waits)


def product_of(key, value):
    return (key.astype(F32) * value.astype(F32)).astype(BF16)


def gate_kernel(per_group, blocks, start_ref, ring_ref, skip_ref, q_ref, k_ref, v_ref, before_ref, *rest):
    out_refs = rest[-blocks:]
    rows, width = out_refs[0].shape
    groups = LANES // per_group
    row = lax.broadcasted_iota(jnp.int32, (rows, rows), 0)
    col = lax.broadcasted_iota(jnp.int32, (rows, rows), 1)
    keep = (row >= col).astype(F32).astype(BF16)
    lane_group = lax.broadcasted_iota(jnp.int32, (2 * rows, blocks * LANES), 1) % LANES // per_group

    def step(t, carry):
        lanes = pl.ds(pl.multiple_of(t * LANES, LANES), LANES)
        spans = [slice(b * rows, (b + 1) * rows) for b in range(blocks)]
        products = [product_of(k_ref[span, lanes], v_ref[span, lanes]) for span in spans]
        before = [before_ref[:, lanes]] + products[:-1]
        data = jnp.concatenate([jnp.concatenate(products, axis=1), jnp.concatenate(before, axis=1)], axis=0)
        rings = ring_ref[pl.ds(pl.multiple_of(t * groups, groups), groups), :]
        left, right = [], []
        for g in range(groups):
            ring = jnp.broadcast_to(rings[g : g + 1, :], (rows, rows))
            ring = pltpu.roll(ring, 0, 1, stride=1, stride_axis=0).astype(BF16)
            lower = ring * keep
            left += [lower, ring - lower]
            right.append(jnp.where(lane_group == g, data, jnp.zeros_like(data)))
        convolved = jnp.dot(
            jnp.concatenate(left, axis=1), jnp.concatenate(right, axis=0), preferred_element_type=F32
        )
        skip = skip_ref[:, lanes]
        for b, span in enumerate(spans):
            here = convolved[:, b * LANES : (b + 1) * LANES] + skip * products[b].astype(F32)
            out_refs[b][:, lanes] = (q_ref[span, lanes].astype(F32) * here).astype(BF16)
        return carry

    lax.fori_loop(0, width // LANES, step, 0)


def gate(rings, skip, queries, key_proj, value_proj, before, start, count, waits=()):
    rows = rings.shape[1]
    seq_len, channels = queries.shape
    blocks = seq_len // rows
    per_group = channels // rings.shape[0]
    tile = min(512, count)
    steps = count // tile

    def at(height):
        return pl.BlockSpec((height, tile), lambda i, s: (0, s[0] * steps + i))

    return pl.pallas_call(
        functools.partial(gate_kernel, per_group, blocks),
        grid_spec=pltpu.PrefetchScalarGridSpec(
            num_scalar_prefetch=1,
            grid=(steps,),
            in_specs=[
                pl.BlockSpec((tile // per_group, rows), lambda i, s: (s[0] * steps + i, 0)),
                at(1),
                at(seq_len),
                at(seq_len),
                at(seq_len),
                pl.BlockSpec((rows, tile), lambda i, s: (0, i)),
            ]
            + [pl.BlockSpec(memory_space=pl.ANY)] * len(waits),
            out_specs=[pl.BlockSpec((rows, tile), lambda i, s: (0, i))] * blocks,
        ),
        out_shape=[jax.ShapeDtypeStruct((rows, count), BF16)] * blocks,
        compiler_params=pltpu.CompilerParams(vmem_limit_bytes=56 << 20),
        cost_estimate=cost(0),
    )(jnp.reshape(start, (1,)).astype(jnp.int32), rings, skip, queries, key_proj, value_proj, before, *waits)


def rings_of(filter_taps):
    return jnp.roll(filter_taps[:, ::-1], 1, axis=1).astype(F32)


def project_kernel(count, weight_count, *refs):
    rows, weights = refs[:count], refs[count : count + weight_count]
    keep_ref, send_ref, total = refs[-3:]
    step = pl.program_id(0)

    @pl.when(step == 0)
    def _():
        total[...] = jnp.zeros_like(total)

    left = jnp.concatenate([r[...] for r in rows], axis=0)
    right = jnp.concatenate([w[...] for w in weights], axis=1)
    total[...] += jnp.dot(left, right, preferred_element_type=F32)

    @pl.when(step == pl.num_programs(0) - 1)
    def _():
        half = total.shape[0] // 2
        keep_ref[...] = total[:half, :]
        send_ref[...] = total[half:, :].astype(BF16)


def project(rows, weights, weight, waits=()):
    depth = rows[0].shape[1]
    height = sum(r.shape[0] for r in rows)
    width = sum(w.shape[1] for w in weights)
    tile = min(1024, depth)
    return pl.pallas_call(
        functools.partial(project_kernel, len(rows), len(weights)),
        grid=(depth // tile,),
        in_specs=[pl.BlockSpec((r.shape[0], tile), lambda k: (0, k)) for r in rows]
        + [pl.BlockSpec((tile, w.shape[1]), lambda k: (k, 0)) for w in weights]
        + [pl.BlockSpec(memory_space=pl.ANY)] * len(waits),
        out_specs=[pl.BlockSpec((height // 2, width), lambda k: (0, 0))] * 2,
        out_shape=[
            jax.ShapeDtypeStruct((height // 2, width), F32),
            jax.ShapeDtypeStruct((height // 2, width), BF16),
        ],
        scratch_shapes=[pltpu.VMEM((height, width), F32)],
        compiler_params=pltpu.CompilerParams(vmem_limit_bytes=40 << 20),
        cost_estimate=cost(weight),
    )(*rows, *weights, *waits)


def settle_kernel(keep_ref, arrived_ref, *refs):
    near_ref, far_ref = refs[-2:]
    rows = near_ref.shape[0]
    near_ref[...] = (keep_ref[:rows, :] + arrived_ref[:rows, :].astype(F32)).astype(BF16)
    far_ref[...] = (keep_ref[rows:, :] + arrived_ref[rows:, :].astype(F32)).astype(BF16)


def settle(keep, arrived, waits):
    rows, width = keep.shape
    tile = min(512, width)
    whole = pl.BlockSpec((rows, tile), lambda i: (0, i))
    return pl.pallas_call(
        settle_kernel,
        grid=(width // tile,),
        in_specs=[whole, whole] + [pl.BlockSpec(memory_space=pl.ANY)] * len(waits),
        out_specs=[pl.BlockSpec((rows // 2, tile), lambda i: (0, i))] * 2,
        out_shape=[jax.ShapeDtypeStruct((rows // 2, width), BF16)] * 2,
        compiler_params=pltpu.CompilerParams(vmem_limit_bytes=16 << 20),
        cost_estimate=cost(0),
    )(keep, arrived, *waits)


def add_kernel(widths, place_ref, *refs):
    total_ref, out_ref = refs[0], refs[-1]
    span = sum(widths)
    for h, width in enumerate(widths):
        for j in range(4):
            start = place_ref[1 + j] * span + sum(widths[:h])
            lanes = pl.ds(pl.multiple_of(start, LANES), width)
            mine = refs[1 + 2 * h + j // 2][:, (j % 2) * width : (j % 2 + 1) * width]
            out_ref[:, lanes] = (total_ref[:, lanes].astype(F32) + mine.astype(F32)).astype(BF16)


def add_slots(residual, total, parts, block, places, slots, order):
    widths = [cut[0].shape[1] // slots // 2 for cut in parts]
    rows = parts[0][0].shape[0]
    span = 4 * sum(widths)
    flat = [(piece, 2 * width) for cut, width in zip(parts, widths) for piece in cut]
    whole = pl.BlockSpec((rows, span), lambda i, s: (block, s[5 + i]))
    so_far = [] if total is None else [total]
    return pl.pallas_call(
        functools.partial(add_kernel, widths),
        grid_spec=pltpu.PrefetchScalarGridSpec(
            num_scalar_prefetch=1,
            grid=(slots,),
            in_specs=[whole]
            + [pl.BlockSpec((rows, w), lambda i, s: (0, i)) for _, w in flat]
            + [pl.BlockSpec(memory_space=pl.ANY)] * len(so_far),
            out_specs=whole,
        ),
        out_shape=jax.ShapeDtypeStruct(residual.shape, residual.dtype),
        input_output_aliases={2 + len(flat): 0} if so_far else {},
        compiler_params=pltpu.CompilerParams(vmem_limit_bytes=16 << 20),
        cost_estimate=cost(1),
    )(jnp.concatenate([jnp.zeros((1,), jnp.int32), order, places]), residual, *[p for p, _ in flat], *so_far)


def swapped(value, bit, devices):
    return lax.ppermute(value, EVERY, [(d, d ^ bit) for d in range(devices)])


def along(value, planes, sources, steps, stride):
    per_window = planes * stride
    pairs = [
        (w * per_window + z * stride + i, w * per_window + (z + steps) * stride + i)
        for w in range(2)
        for z in sources
        for i in range(stride)
    ]
    return lax.ppermute(value, EVERY, pairs)


def arrivals(planes):
    return [
        [(way, s) for s in range(1, planes) for way in (1, -1) if 0 <= z + way * s < planes]
        for z in range(planes)
    ]


def paired(queries, key_proj, value_proj, filter_taps, skip_gain, out_weight, residual):
    seq_len, channels = queries.shape
    rows = filter_taps.shape[1]
    blocks = seq_len // rows
    half = channels // 2
    devices = 2 * lax.axis_size("seq") * 2
    window, section = lax.axis_index("groups"), lax.axis_index("section")
    planes = lax.axis_size("seq") // 2
    plane, side = lax.axis_index("seq") // 2, lax.axis_index("seq") % 2

    last = seq_len - rows
    shards = planes * 4
    edge = [w * shards + i for w in range(2) for i in range(shards - 1)]
    turn = [i for i in edge if i % 4 == 3]

    def outgoing(start):
        return product_of(
            lax.dynamic_slice(key_proj, (last, start), (rows, half)),
            lax.dynamic_slice(value_proj, (last, start), (rows, half)),
        )

    before_own = lax.ppermute(outgoing(window * half), EVERY, [(i, i + 1) for i in edge])
    leaving = outgoing((1 - window) * half)
    before_theirs = lax.ppermute(leaving, EVERY, [(i, i + 1) for i in edge if i not in turn])
    passing = lax.ppermute(leaving, EVERY, [(i, i - 2) for i in turn])
    passing = lax.ppermute(passing, EVERY, [(i - 2, i + 1) for i in turn])
    before_theirs = jnp.where(side + section == 0, passing, before_theirs)

    mine = lax.dynamic_slice_in_dim(out_weight, window * half, half, 0)
    cuts = [mine[:, : mine.shape[1] // 2], mine[:, mine.shape[1] // 2 :]]
    got = [{}, {}]
    ends = [[c, c] for c in cuts]

    def hold(cuts_held, s, *waits):
        held = after([v for cut in cuts_held for v in ends[cut]], *waits)
        for n, cut in enumerate(cuts_held):
            ends[cut] = held[2 * n : 2 * n + 2]
            got[cut][-1, s], got[cut][1, s] = ends[cut]

    def forward(cut, s):
        up, down = ends[cut]
        up = along(up, planes, range(s - 1, planes - 1), 1, 4)
        down = along(down, planes, range(1, planes - s + 1), -1, 4)
        got[cut][1, s], got[cut][-1, s] = down, up
        ends[cut] = [up, down]

    forward(0, 1)
    forward(1, 1)
    order = arrivals(planes)

    def slot(cut, j):
        value = got[cut][order[0][j]]
        for z in range(1, planes):
            value = jnp.where(plane == z, got[cut][order[z][j]], value)
        return value

    def slot_place(j):
        return sum(jnp.where(plane == z, z + order[z][j][0] * order[z][j][1], 0) for z in range(planes))

    rings, skip = rings_of(filter_taps), skip_gain[None, :]
    args = (rings, skip, queries, key_proj, value_proj)
    firsts = gate(*args, before_own, window, half)[::-1]
    crossed = [swapped(f, 2, devices) for f in firsts]
    theirs = gate(*args, before_theirs, 1 - window, half, firsts)[::-1]
    seconds = [swapped(t, devices // 2, devices) for t in theirs]
    hold([0, 1], 1, *theirs)
    forward(0, 2)
    forward(1, 2)
    marker = after([jnp.zeros((8, LANES), F32)], crossed[0], weight=1)
    for s in range(3, planes):
        hold([0], s - 1, *marker)
        forward(0, s)
        hold([1], s - 1, crossed[-1], seconds[0])
        forward(1, s)
    far = [swapped(o, 2, devices) for o in seconds]
    gathered = list(zip(firsts, crossed, seconds, far))

    def sent_back(send):
        return swapped(send, devices // 2, devices)

    def shared(keep, arrived, *waits):
        near, far_rows = settle(keep, arrived, waits)
        return [near, swapped(far_rows, 2, devices)]

    def both(value):
        return [value, swapped(value, 1, devices)]

    place = jnp.stack([side * 2 + section, side * 2 + 1 - section, 2 - side * 2 + section, 3 - side * 2 - section])
    place = place.astype(jnp.int32)
    early = both(mine)
    for j in range(planes - 2):
        pairs = [both(slot(cut, j)) for cut in range(2)]
        early += [pairs[0][0], pairs[1][0], pairs[0][1], pairs[1][1]]
    early_places = jnp.stack([plane] + [slot_place(j) for j in range(planes - 2)]).astype(jnp.int32)
    total, sends, arrivals_back = None, [], []
    last_slots = []
    for i, block in enumerate(reversed(range(blocks))):
        keep, send = project(gathered[i], early, 1 if i else 2, sends[-1:])
        sends.append(send)
        arrivals_back.append(sent_back(send))
        total = add_slots(residual, total, [shared(keep, arrivals_back[-1])], block, early_places, planes - 1, place)
        if i < 2:
            hold([i], planes - 1, far[i], send)
            last_slots.append(both(slot(i, planes - 2)))
    everyone = [gathered[blocks - 1 - b][p] for p in range(4) for b in range(blocks)]
    late = []
    for cut in range(2):
        keep, send = project(everyone, last_slots[cut], 4, [sends[-1], arrivals_back[cut]])
        sends.append(send)
        late.append(shared(keep, sent_back(send), *([total] if cut else [])))
    return add_slots(residual, total, late, 0, slot_place(planes - 2)[None].astype(jnp.int32), 1, place)


def general(queries, key_proj, value_proj, filter_taps, skip_gain, out_weight, residual):
    seq_len, channels = queries.shape
    rows = filter_taps.shape[1]
    outgoing = product_of(key_proj[seq_len - rows :], value_proj[seq_len - rows :])
    count = lax.axis_size(SEQ)
    before = lax.ppermute(outgoing, SEQ, [(i, i + 1) for i in range(count - 1)])
    rings, skip = rings_of(filter_taps), skip_gain[None, :]
    gated = gate(rings, skip, queries, key_proj, value_proj, before, jnp.int32(0), channels)
    gated = jnp.concatenate(gated, axis=0)
    weight = lax.all_gather(out_weight, SEQ, axis=1, tiled=True)
    projected = jnp.dot(gated, weight, preferred_element_type=F32)
    share = lax.psum_scatter(projected, "chan", scatter_dimension=1, tiled=True)
    return (residual.astype(F32) + share).astype(BF16)


def solution(mesh):
    sizes = mesh.shape
    fits = sizes["groups"] == 2 and sizes["chan"] == 1 and sizes["section"] == 2 and sizes["seq"] % 2 == 0
    return jax.shard_map(
        paired if fits and sizes["seq"] >= 6 else general,
        mesh=mesh,
        in_specs=(
            P(("groups", "seq", "section"), "chan"),
            P(("groups", "seq", "section"), "chan"),
            P(("groups", "seq", "section"), "chan"),
            P("chan", None),
            P("chan"),
            P("chan", ("seq", "section")),
            P(("groups", "seq", "section"), "chan"),
        ),
        out_specs=P(("groups", "seq", "section"), "chan"),
        check_vma=False,
    )
```

```python
import functools

import jax
import jax.numpy as jnp
from jax import lax
from jax.experimental import pallas as pl
from jax.experimental.pallas import tpu as pltpu
from jax.sharding import PartitionSpec as P

LANES = 128
SEQ = ("seq", "section")
EVERY = ("groups", "seq", "section")
F32, BF16 = jnp.float32, jnp.bfloat16


def cost(us):
    return pl.CostEstimate(flops=int(us * 1.1e9), bytes_accessed=1, transcendentals=0)


def pass_kernel(*refs):
    pass


def after(values, *waits, weight=0):
    return pl.pallas_call(
        pass_kernel,
        in_specs=[pl.BlockSpec(memory_space=pl.ANY)] * (len(values) + len(waits)),
        out_specs=[pl.BlockSpec(memory_space=pl.ANY)] * len(values),
        out_shape=[jax.ShapeDtypeStruct(v.shape, v.dtype) for v in values],
        input_output_aliases={i: i for i in range(len(values))},
        cost_estimate=cost(weight),
    )(*values, *waits)


def pick_kernel(count, which_ref, *refs):
    outs = refs[count:]
    part = outs[0].shape[1]
    for n, ref in enumerate(refs[:count]):

        @pl.when(which_ref[0] == n)
        def _():
            for i, out in enumerate(outs):
                out[...] = ref[:, i * part : (i + 1) * part]


def pick(choices, which, rows, parts=1):
    width = choices[0].shape[1]
    part = width // parts
    tile = min(1024, rows)

    def block_of(n):
        return pl.BlockSpec((tile, width), lambda i, s: (jnp.where(s[0] == n, i, 0), 0))

    return pl.pallas_call(
        functools.partial(pick_kernel, len(choices)),
        grid_spec=pltpu.PrefetchScalarGridSpec(
            num_scalar_prefetch=1,
            grid=(rows // tile,),
            in_specs=[block_of(n) for n in range(len(choices))],
            out_specs=[pl.BlockSpec((tile, part), lambda i, s: (i, 0))] * parts,
        ),
        out_shape=[jax.ShapeDtypeStruct((rows, part), choices[0].dtype)] * parts,
        compiler_params=pltpu.CompilerParams(vmem_limit_bytes=16 << 20),
        cost_estimate=cost(0.1),
    )(jnp.reshape(which, (1,)).astype(jnp.int32), *choices)


def product_of(key, value):
    return (key.astype(F32) * value.astype(F32)).astype(BF16)


def gate_kernel(per_group, blocks, start_ref, ring_ref, skip_ref, q_ref, k_ref, v_ref, before_ref, *rest):
    out_refs = rest[-blocks:]
    rows, width = out_refs[0].shape
    groups = LANES // per_group
    row = lax.broadcasted_iota(jnp.int32, (rows, rows), 0)
    col = lax.broadcasted_iota(jnp.int32, (rows, rows), 1)
    keep = (row >= col).astype(F32).astype(BF16)
    lane_group = lax.broadcasted_iota(jnp.int32, (2 * rows, blocks * LANES), 1) % LANES // per_group

    def step(t, carry):
        lanes = pl.ds(pl.multiple_of(t * LANES, LANES), LANES)
        spans = [slice(b * rows, (b + 1) * rows) for b in range(blocks)]
        products = [product_of(k_ref[span, lanes], v_ref[span, lanes]) for span in spans]
        before = [before_ref[:, lanes]] + products[:-1]
        data = jnp.concatenate([jnp.concatenate(products, axis=1), jnp.concatenate(before, axis=1)], axis=0)
        rings = ring_ref[pl.ds(pl.multiple_of(t * groups, groups), groups), :]
        left, right = [], []
        for g in range(groups):
            ring = jnp.broadcast_to(rings[g : g + 1, :], (rows, rows))
            ring = pltpu.roll(ring, 0, 1, stride=1, stride_axis=0).astype(BF16)
            lower = ring * keep
            left += [lower, ring - lower]
            right.append(jnp.where(lane_group == g, data, jnp.zeros_like(data)))
        convolved = jnp.dot(
            jnp.concatenate(left, axis=1), jnp.concatenate(right, axis=0), preferred_element_type=F32
        )
        skip = skip_ref[:, lanes]
        for b, span in enumerate(spans):
            here = convolved[:, b * LANES : (b + 1) * LANES] + skip * products[b].astype(F32)
            out_refs[b][:, lanes] = (q_ref[span, lanes].astype(F32) * here).astype(BF16)
        return carry

    lax.fori_loop(0, width // LANES, step, 0)


def gate(rings, skip, queries, key_proj, value_proj, before, start, count, waits=()):
    rows = rings.shape[1]
    seq_len, channels = queries.shape
    blocks = seq_len // rows
    per_group = channels // rings.shape[0]
    tile = min(512, count)
    steps = count // tile

    def at(height):
        return pl.BlockSpec((height, tile), lambda i, s: (0, s[0] * steps + i))

    return pl.pallas_call(
        functools.partial(gate_kernel, per_group, blocks),
        grid_spec=pltpu.PrefetchScalarGridSpec(
            num_scalar_prefetch=1,
            grid=(steps,),
            in_specs=[
                pl.BlockSpec((tile // per_group, rows), lambda i, s: (s[0] * steps + i, 0)),
                at(1),
                at(seq_len),
                at(seq_len),
                at(seq_len),
                pl.BlockSpec((rows, tile), lambda i, s: (0, i)),
            ]
            + [pl.BlockSpec(memory_space=pl.ANY)] * len(waits),
            out_specs=[pl.BlockSpec((rows, tile), lambda i, s: (0, i))] * blocks,
        ),
        out_shape=[jax.ShapeDtypeStruct((rows, count), BF16)] * blocks,
        compiler_params=pltpu.CompilerParams(vmem_limit_bytes=60 << 20),
        cost_estimate=cost(0.1),
    )(jnp.reshape(start, (1,)).astype(jnp.int32), rings, skip, queries, key_proj, value_proj, before, *waits)


def rings_of(filter_taps):
    return jnp.roll(filter_taps[:, ::-1], 1, axis=1).astype(F32)


def project_kernel(row_count, choices, weight_count, outs, which_ref, *refs):
    rows, weights = refs[:row_count], refs[row_count : row_count + choices * weight_count]
    out_refs, total = refs[-1 - outs : -1], refs[-1]
    step = pl.program_id(0)

    @pl.when(step == 0)
    def _():
        total[...] = jnp.zeros_like(total)

    left = jnp.concatenate([r[...] for r in rows], axis=0)
    for n in range(choices):

        @pl.when(which_ref[0] == n)
        def _():
            right = jnp.concatenate([w[...] for w in weights[n::choices]], axis=1)
            total[...] += jnp.dot(left, right, preferred_element_type=F32)

    @pl.when(step == pl.num_programs(0) - 1)
    def _():
        part = out_refs[0].shape[0]
        for i, out_ref in enumerate(out_refs):
            out_ref[...] = total[i * part : (i + 1) * part, :].astype(out_ref.dtype)


def project(rows, weights, dtypes, waits=(), which=0):
    depth = rows[0].shape[1]
    height = sum(r.shape[0] for r in rows)
    widths = [w[0].shape[1] for w in weights]
    tile = min(1024, depth)
    choices = len(weights[0])

    def weight_spec(width, n):
        if choices == 1:
            return pl.BlockSpec((tile, width), lambda k, s: (k, 0))
        return pl.BlockSpec((tile, width), lambda k, s: (jnp.where(s[0] == n, k, 0), 0))

    part = (height // len(dtypes), sum(widths))
    return pl.pallas_call(
        functools.partial(project_kernel, len(rows), choices, len(weights), len(dtypes)),
        grid_spec=pltpu.PrefetchScalarGridSpec(
            num_scalar_prefetch=1,
            grid=(depth // tile,),
            in_specs=[pl.BlockSpec((r.shape[0], tile), lambda k, s: (0, k)) for r in rows]
            + [weight_spec(width, n) for width in widths for n in range(choices)]
            + [pl.BlockSpec(memory_space=pl.ANY)] * len(waits),
            out_specs=[pl.BlockSpec(part, lambda k, s: (0, 0))] * len(dtypes),
            scratch_shapes=[pltpu.VMEM((height, sum(widths)), F32)],
        ),
        out_shape=[jax.ShapeDtypeStruct(part, dtype) for dtype in dtypes],
        compiler_params=pltpu.CompilerParams(vmem_limit_bytes=60 << 20),
        cost_estimate=cost(1),
    )(jnp.full((1,), which, jnp.int32), *rows, *[w for group in weights for w in group], *waits)


def settle_kernel(keep_ref, arrived_ref, *refs):
    near_ref, far_ref = refs[-2:]
    rows = near_ref.shape[0]
    near_ref[...] = (keep_ref[:rows, :] + arrived_ref[:rows, :].astype(F32)).astype(BF16)
    far_ref[...] = (keep_ref[rows:, :] + arrived_ref[rows:, :].astype(F32)).astype(BF16)


def settle(keep, arrived, waits):
    rows, width = keep.shape
    tile = min(512, width)
    whole = pl.BlockSpec((rows, tile), lambda i: (0, i))
    return pl.pallas_call(
        settle_kernel,
        grid=(width // tile,),
        in_specs=[whole, whole] + [pl.BlockSpec(memory_space=pl.ANY)] * len(waits),
        out_specs=[pl.BlockSpec((rows // 2, tile), lambda i: (0, i))] * 2,
        out_shape=[jax.ShapeDtypeStruct((rows // 2, width), BF16)] * 2,
        compiler_params=pltpu.CompilerParams(vmem_limit_bytes=16 << 20),
        cost_estimate=cost(0),
    )(keep, arrived, *waits)


def add_kernel(widths, place_ref, *refs):
    total_ref, out_ref = refs[0], refs[-1]
    span = sum(widths)
    for h, width in enumerate(widths):
        for j in range(4):
            start = place_ref[1 + j] * span + sum(widths[:h])
            lanes = pl.ds(pl.multiple_of(start, LANES), width)
            mine = refs[1 + 2 * h + j // 2][:, (j % 2) * width : (j % 2 + 1) * width]
            out_ref[:, lanes] = (total_ref[:, lanes].astype(F32) + mine.astype(F32)).astype(BF16)


def add_slots(residual, total, parts, block, places, slots, order):
    widths = [cut[0].shape[1] // slots // 2 for cut in parts]
    rows = parts[0][0].shape[0]
    span = 4 * sum(widths)
    flat = [(piece, 2 * width) for cut, width in zip(parts, widths) for piece in cut]
    whole = pl.BlockSpec((rows, span), lambda i, s: (block, s[5 + i]))
    so_far = [] if total is None else [total]
    return pl.pallas_call(
        functools.partial(add_kernel, widths),
        grid_spec=pltpu.PrefetchScalarGridSpec(
            num_scalar_prefetch=1,
            grid=(slots,),
            in_specs=[whole]
            + [pl.BlockSpec((rows, w), lambda i, s: (0, i)) for _, w in flat]
            + [pl.BlockSpec(memory_space=pl.ANY)] * len(so_far),
            out_specs=whole,
        ),
        out_shape=jax.ShapeDtypeStruct(residual.shape, residual.dtype),
        input_output_aliases={2 + len(flat): 0} if so_far else {},
        compiler_params=pltpu.CompilerParams(vmem_limit_bytes=16 << 20),
        cost_estimate=cost(1),
    )(jnp.concatenate([jnp.zeros((1,), jnp.int32), order, places]), residual, *[p for p, _ in flat], *so_far)


def swapped(value, bit, devices):
    return lax.ppermute(value, EVERY, [(d, d ^ bit) for d in range(devices)])


def along(value, planes, sources, steps, stride):
    per_window = planes * stride
    pairs = [
        (w * per_window + z * stride + i, w * per_window + (z + steps) * stride + i)
        for w in range(2)
        for z in sources
        for i in range(stride)
    ]
    return lax.ppermute(value, EVERY, pairs)


def arrivals(planes):
    return [
        [(way, s) for s in range(1, planes) for way in (1, -1) if 0 <= z + way * s < planes]
        for z in range(planes)
    ]


def paired(queries, key_proj, value_proj, filter_taps, skip_gain, out_weight, residual):
    seq_len, channels = queries.shape
    rows = filter_taps.shape[1]
    blocks = seq_len // rows
    half = channels // 2
    devices = 2 * lax.axis_size("seq") * 2
    window, section = lax.axis_index("groups"), lax.axis_index("section")
    planes = lax.axis_size("seq") // 2
    plane, side = lax.axis_index("seq") // 2, lax.axis_index("seq") % 2

    last = seq_len - rows
    shards = planes * 4
    edge = [(w * shards + i, w * shards + i + 1) for w in range(2) for i in range(shards - 1)]

    def outgoing(start, spare):
        product = product_of(
            lax.dynamic_slice(key_proj, (last, start), (rows, half)),
            lax.dynamic_slice(value_proj, (last, start), (rows, half)),
        )
        return jnp.pad(product, ((0, spare), (0, 0)))

    before_own = lax.ppermute(outgoing(window * half, 32), EVERY, edge)
    before_theirs = lax.ppermute(outgoing((1 - window) * half, 16), EVERY, edge)

    mine = lax.dynamic_slice_in_dim(out_weight, window * half, half, 0)
    (mine,) = after([mine], before_own)
    got = {}

    def forward(s, up, down):
        got[-1, s] = along(up, planes, range(s - 1, planes - 1), 1, 4)
        got[1, s] = along(down, planes, range(1, planes - s + 1), -1, 4)

    def hold(s, *waits):
        got[-1, s], got[1, s] = after([got[-1, s], got[1, s]], *waits)

    def chosen(j, among, parts=1):
        names = sorted({order[z][j] for z in among})
        which = sum(jnp.where(plane == z, names.index(order[z][j]), 0) for z in among)
        return pick([got[name] for name in names], which, half, parts)

    def slot_place(j):
        return sum(jnp.where(plane == z, z + order[z][j][0] * order[z][j][1], 0) for z in range(planes))

    def both(value):
        return [value, swapped(value, 1, devices)]

    order = arrivals(planes)
    everywhere, inner = list(range(planes)), list(range(1, planes - 1))
    forward(1, mine, mine)
    early = both(mine)

    rings, skip = rings_of(filter_taps), skip_gain[None, :]
    args = (rings, skip, queries, key_proj, value_proj)
    firsts = gate(*args, before_own, window, half)[::-1]
    crossed = [swapped(f, 2, devices) for f in firsts]
    theirs = gate(*args, before_theirs, 1 - window, half, [*firsts, early[1]])[::-1]
    hold(1, *theirs)
    seconds = [swapped(theirs[0], devices // 2, devices)]
    for t in theirs[1:]:
        seconds += [swapped(*after([t], crossed[0]), devices // 2, devices)]
    far = [swapped(o, 2, devices) for o in seconds]
    for s in range(2, planes - 1):
        forward(s, got[-1, s - 1], got[1, s - 1])
        early += both(*after(chosen(s - 2, everywhere), seconds[0], crossed[-1]))
        hold(s, far[0], seconds[-1])
    gathered = list(zip(firsts, crossed, seconds, far))

    (middle,) = after(chosen(planes - 2, inner), early[-1])
    to_ends = [(w * shards + p * 4 + i, w * shards + q * 4 + i) for w in range(2) for i in range(4)
               for p, q in ((1, 0), (planes - 2, planes - 1))]
    last_arrived = lax.ppermute(middle, EVERY, to_ends)
    at_end = jnp.where((plane == 0) | (plane == planes - 1), 0, 1)

    def sent_back(send):
        return swapped(send, devices // 2, devices)

    def shared(keep, arrived, *waits):
        near, far_rows = settle(keep, arrived, waits)
        return [near, swapped(far_rows, 2, devices)]

    place = jnp.stack([side * 2 + section, side * 2 + 1 - section, 2 - side * 2 + section, 3 - side * 2 - section])
    place = place.astype(jnp.int32)
    def places(slots):
        return jnp.stack([slot_place(j) if j >= 0 else plane for j in slots]).astype(jnp.int32)

    sums = []

    def summed(rows, weights):
        keep, send = project(rows, weights, [F32, BF16], [v for _, v, _ in sums[-1:]])
        sums.append((keep, send, sent_back(send)))

    single = [[w] for w in early]
    for pieces in gathered:
        summed(pieces, single)
    halves = [both(cut) for cut in chosen(planes - 3, everywhere, 2)]
    everyone = [gathered[blocks - 1 - b][p] for p in range(4) for b in range(blocks)]
    summed(everyone, [[pair[c]] for c in range(2) for pair in halves])
    parts = [shared(keep, arrived) for keep, _, arrived in sums]

    middle = both(middle)
    last_arrived = both(*after([last_arrived], parts[0][1], sums[blocks - 1][2], sums[blocks][1], middle[1]))
    ends = list(zip(last_arrived, middle))
    (send,) = project(everyone[2 * blocks :], ends, [BF16], [], at_end)
    (keep,) = project(everyone[: 2 * blocks], ends, [F32], [send], at_end)

    total = None
    for i, block in enumerate(reversed(range(blocks))):
        total = add_slots(residual, total, [parts[i]], block, places(range(-1, planes - 3)), planes - 2, place)
    total = add_slots(residual, total, [parts[blocks]], 0, places([planes - 3]), 1, place)
    last_part = shared(keep, sent_back(send), total)
    return add_slots(residual, total, [last_part], 0, places([planes - 2]), 1, place)


def general(queries, key_proj, value_proj, filter_taps, skip_gain, out_weight, residual):
    seq_len, channels = queries.shape
    rows = filter_taps.shape[1]
    outgoing = product_of(key_proj[seq_len - rows :], value_proj[seq_len - rows :])
    count = lax.axis_size(SEQ)
    before = lax.ppermute(outgoing, SEQ, [(i, i + 1) for i in range(count - 1)])
    rings, skip = rings_of(filter_taps), skip_gain[None, :]
    gated = gate(rings, skip, queries, key_proj, value_proj, before, jnp.int32(0), channels)
    gated = jnp.concatenate(gated, axis=0)
    weight = lax.all_gather(out_weight, SEQ, axis=1, tiled=True)
    projected = jnp.dot(gated, weight, preferred_element_type=F32)
    share = lax.psum_scatter(projected, "chan", scatter_dimension=1, tiled=True)
    return (residual.astype(F32) + share).astype(BF16)


def solution(mesh):
    sizes = mesh.shape
    fits = sizes["groups"] == 2 and sizes["chan"] == 1 and sizes["section"] == 2 and sizes["seq"] % 2 == 0
    return jax.shard_map(
        paired if fits and sizes["seq"] >= 8 else general,
        mesh=mesh,
        in_specs=(
            P(("groups", "seq", "section"), "chan"),
            P(("groups", "seq", "section"), "chan"),
            P(("groups", "seq", "section"), "chan"),
            P("chan", None),
            P("chan"),
            P("chan", ("seq", "section")),
            P(("groups", "seq", "section"), "chan"),
        ),
        out_specs=P(("groups", "seq", "section"), "chan"),
        check_vma=False,
    )
```

```python
import functools

import jax
import jax.numpy as jnp
from jax import lax
from jax.experimental import pallas as pl
from jax.experimental.pallas import tpu as pltpu
from jax.sharding import PartitionSpec as P

LANES = 128
SEQ = ("seq", "section")
EVERY = ("groups", "seq", "section")
F32, BF16 = jnp.float32, jnp.bfloat16


def cost(us):
    return pl.CostEstimate(flops=int(us * 1.1e9), bytes_accessed=1, transcendentals=0)


def pass_kernel(*refs):
    pass


def after(values, *waits, weight=0):
    return pl.pallas_call(
        pass_kernel,
        in_specs=[pl.BlockSpec(memory_space=pl.ANY)] * (len(values) + len(waits)),
        out_specs=[pl.BlockSpec(memory_space=pl.ANY)] * len(values),
        out_shape=[jax.ShapeDtypeStruct(v.shape, v.dtype) for v in values],
        input_output_aliases={i: i for i in range(len(values))},
        compiler_params=pltpu.CompilerParams(vmem_limit_bytes=60 << 20),
        cost_estimate=cost(weight),
    )(*values, *waits)


def product_of(key, value):
    return (key.astype(F32) * value.astype(F32)).astype(BF16)


def gate_kernel(per_group, blocks, start_ref, ring_ref, skip_ref, q_ref, k_ref, v_ref, before_ref, *rest):
    out_refs = rest[-blocks:]
    rows, width = out_refs[0].shape
    groups = LANES // per_group
    row = lax.broadcasted_iota(jnp.int32, (rows, rows), 0)
    col = lax.broadcasted_iota(jnp.int32, (rows, rows), 1)
    keep = (row >= col).astype(F32).astype(BF16)
    lane_group = lax.broadcasted_iota(jnp.int32, (2 * rows, blocks * LANES), 1) % LANES // per_group

    def step(t, carry):
        lanes = pl.ds(pl.multiple_of(t * LANES, LANES), LANES)
        spans = [slice(b * rows, (b + 1) * rows) for b in range(blocks)]
        products = [product_of(k_ref[span, lanes], v_ref[span, lanes]) for span in spans]
        before = [before_ref[:, lanes]] + products[:-1]
        data = jnp.concatenate([jnp.concatenate(products, axis=1), jnp.concatenate(before, axis=1)], axis=0)
        rings = ring_ref[pl.ds(pl.multiple_of(t * groups, groups), groups), :]
        left, right = [], []
        for g in range(groups):
            ring = jnp.broadcast_to(rings[g : g + 1, :], (rows, rows))
            ring = pltpu.roll(ring, 0, 1, stride=1, stride_axis=0).astype(BF16)
            lower = ring * keep
            left += [lower, ring - lower]
            right.append(jnp.where(lane_group == g, data, jnp.zeros_like(data)))
        convolved = jnp.dot(
            jnp.concatenate(left, axis=1), jnp.concatenate(right, axis=0), preferred_element_type=F32
        )
        skip = skip_ref[:, lanes]
        for b, span in enumerate(spans):
            here = convolved[:, b * LANES : (b + 1) * LANES] + skip * products[b].astype(F32)
            out_refs[b][:, lanes] = (q_ref[span, lanes].astype(F32) * here).astype(BF16)
        return carry

    lax.fori_loop(0, width // LANES, step, 0)


def gate(rings, skip, queries, key_proj, value_proj, before, start, count, waits=()):
    rows = rings.shape[1]
    seq_len, channels = queries.shape
    blocks = seq_len // rows
    per_group = channels // rings.shape[0]
    tile = min(512, count)
    steps = count // tile

    def at(height):
        return pl.BlockSpec((height, tile), lambda i, s: (0, s[0] * steps + i))

    return pl.pallas_call(
        functools.partial(gate_kernel, per_group, blocks),
        grid_spec=pltpu.PrefetchScalarGridSpec(
            num_scalar_prefetch=1,
            grid=(steps,),
            in_specs=[
                pl.BlockSpec((tile // per_group, rows), lambda i, s: (s[0] * steps + i, 0)),
                at(1),
                at(seq_len),
                at(seq_len),
                at(seq_len),
                pl.BlockSpec((rows, tile), lambda i, s: (0, i)),
            ]
            + [pl.BlockSpec(memory_space=pl.ANY)] * len(waits),
            out_specs=[pl.BlockSpec((rows, tile), lambda i, s: (0, i))] * blocks,
        ),
        out_shape=[jax.ShapeDtypeStruct((rows, count), BF16)] * blocks,
        compiler_params=pltpu.CompilerParams(vmem_limit_bytes=60 << 20),
        cost_estimate=cost(0.1),
    )(jnp.reshape(start, (1,)).astype(jnp.int32), rings, skip, queries, key_proj, value_proj, before, *waits)


def rings_of(filter_taps):
    return jnp.roll(filter_taps[:, ::-1], 1, axis=1).astype(F32)


def project_kernel(row_count, choices, weight_count, outs, which_ref, *refs):
    rows, weights = refs[:row_count], refs[row_count : row_count + choices * weight_count]
    out_refs, total = refs[-1 - outs : -1], refs[-1]
    step = pl.program_id(0)

    @pl.when(step == 0)
    def _():
        total[...] = jnp.zeros_like(total)

    left = jnp.concatenate([r[...] for r in rows], axis=0)
    for n in range(choices):

        @pl.when(which_ref[0] == n)
        def _():
            right = jnp.concatenate([w[...] for w in weights[n::choices]], axis=1)
            total[...] += jnp.dot(left, right, preferred_element_type=F32)

    @pl.when(step == pl.num_programs(0) - 1)
    def _():
        part = out_refs[0].shape[0]
        for i, out_ref in enumerate(out_refs):
            out_ref[...] = total[i * part : (i + 1) * part, :].astype(out_ref.dtype)


def project(rows, weights, dtypes, waits=(), which=0):
    depth = rows[0].shape[1]
    height = sum(r.shape[0] for r in rows)
    widths = [w[0].shape[1] for w in weights]
    tile = min(1024, depth)
    choices = len(weights[0])

    def weight_spec(width, n):
        if choices == 1:
            return pl.BlockSpec((tile, width), lambda k, s: (k, 0))
        return pl.BlockSpec((tile, width), lambda k, s: (jnp.where(s[0] == n, k, 0), 0))

    part = (height // len(dtypes), sum(widths))
    return pl.pallas_call(
        functools.partial(project_kernel, len(rows), choices, len(weights), len(dtypes)),
        grid_spec=pltpu.PrefetchScalarGridSpec(
            num_scalar_prefetch=1,
            grid=(depth // tile,),
            in_specs=[pl.BlockSpec((r.shape[0], tile), lambda k, s: (0, k)) for r in rows]
            + [weight_spec(width, n) for width in widths for n in range(choices)]
            + [pl.BlockSpec(memory_space=pl.ANY)] * len(waits),
            out_specs=[pl.BlockSpec(part, lambda k, s: (0, 0))] * len(dtypes),
            scratch_shapes=[pltpu.VMEM((height, sum(widths)), F32)],
        ),
        out_shape=[jax.ShapeDtypeStruct(part, dtype) for dtype in dtypes],
        compiler_params=pltpu.CompilerParams(vmem_limit_bytes=60 << 20),
        cost_estimate=cost(1),
    )(jnp.full((1,), which, jnp.int32), *rows, *[w for group in weights for w in group], *waits)


def settle_kernel(keep_ref, arrived_ref, *refs):
    near_ref, far_ref = refs[-2:]
    rows = near_ref.shape[0]
    near_ref[...] = (keep_ref[:rows, :] + arrived_ref[:rows, :].astype(F32)).astype(BF16)
    far_ref[...] = (keep_ref[rows:, :] + arrived_ref[rows:, :].astype(F32)).astype(BF16)


def settle(keep, arrived, waits=()):
    rows, width = keep.shape
    tile = min(512, width)
    whole = pl.BlockSpec((rows, tile), lambda i: (0, i))
    return pl.pallas_call(
        settle_kernel,
        grid=(width // tile,),
        in_specs=[whole, whole] + [pl.BlockSpec(memory_space=pl.ANY)] * len(waits),
        out_specs=[pl.BlockSpec((rows // 2, tile), lambda i: (0, i))] * 2,
        out_shape=[jax.ShapeDtypeStruct((rows // 2, width), BF16)] * 2,
        compiler_params=pltpu.CompilerParams(vmem_limit_bytes=60 << 20),
        cost_estimate=cost(0),
    )(keep, arrived, *waits)


def add_kernel(widths, place_ref, *refs):
    total_ref, out_ref = refs[0], refs[-1]
    span = sum(widths)
    for h, width in enumerate(widths):
        for j in range(4):
            start = place_ref[j] * span + sum(widths[:h])
            lanes = pl.ds(pl.multiple_of(start, LANES), width)
            mine = refs[1 + 2 * h + j // 2][:, (j % 2) * width : (j % 2 + 1) * width]
            out_ref[:, lanes] = (total_ref[:, lanes].astype(F32) + mine.astype(F32)).astype(BF16)


def add_slots(residual, total, parts, block, place, first, slots, waits=()):
    widths = [cut[0].shape[1] // slots // 2 for cut in parts]
    rows = parts[0][0].shape[0]
    span = 4 * sum(widths)
    flat = [(piece, 2 * width) for cut, width in zip(parts, widths) for piece in cut]
    whole = pl.BlockSpec((rows, span), lambda i, s: (block, s[4 + first + i]))
    so_far = ([] if total is None else [total]) + list(waits)
    return pl.pallas_call(
        functools.partial(add_kernel, widths),
        grid_spec=pltpu.PrefetchScalarGridSpec(
            num_scalar_prefetch=1,
            grid=(slots,),
            in_specs=[whole]
            + [pl.BlockSpec((rows, w), lambda i, s: (0, i)) for _, w in flat]
            + [pl.BlockSpec(memory_space=pl.ANY)] * len(so_far),
            out_specs=whole,
        ),
        out_shape=jax.ShapeDtypeStruct(residual.shape, residual.dtype),
        input_output_aliases={} if total is None else {2 + len(flat): 0},
        compiler_params=pltpu.CompilerParams(vmem_limit_bytes=60 << 20),
        cost_estimate=cost(1),
    )(place, residual, *[p for p, _ in flat], *so_far)


def swapped(value, bit, devices):
    return lax.ppermute(value, EVERY, [(d, d ^ bit) for d in range(devices)])


def paired(queries, key_proj, value_proj, filter_taps, skip_gain, out_weight, residual):
    seq_len, channels = queries.shape
    rows = filter_taps.shape[1]
    blocks = seq_len // rows
    half = channels // 2
    devices = 2 * lax.axis_size("seq") * 2
    window, section = lax.axis_index("groups"), lax.axis_index("section")
    planes = lax.axis_size("seq") // 2
    plane, side = lax.axis_index("seq") // 2, lax.axis_index("seq") % 2

    last = seq_len - rows
    shards = planes * 4
    edge = [(w * shards + i, w * shards + i + 1) for w in range(2) for i in range(shards - 1)]

    def outgoing(start, spare):
        product = product_of(
            lax.dynamic_slice(key_proj, (last, start), (rows, half)),
            lax.dynamic_slice(value_proj, (last, start), (rows, half)),
        )
        return jnp.pad(product, ((0, spare), (0, 0)))

    before_own = lax.ppermute(outgoing(window * half, 0), EVERY, edge)
    before_theirs = lax.ppermute(outgoing((1 - window) * half, 16), EVERY, [(p, q ^ 1) for p, q in edge])

    def step(value, *pairs):
        return lax.ppermute(
            value, EVERY, [(w * shards + p * 4 + i, w * shards + q * 4 + i) for w in range(2) for p, q in pairs for i in range(4)]
        )

    def both(value):
        return [value, swapped(value, 1, devices)]

    mine = lax.dynamic_slice_in_dim(out_weight, window * half, half, 0)
    rings, skip = rings_of(filter_taps), skip_gain[None, :]
    order = [side * 2 + section, side * 2 + 1 - section, 2 - side * 2 + section, 3 - side * 2 - section]
    slots = [[0, 1, 2, 3], [1, 0, 3, 2], [2, 2, 1, 1], [3, 3, 0, 0]]
    held = [sum(jnp.where(plane == z, p, 0) for z, p in enumerate(slot)) for slot in slots]
    place = jnp.stack(order + held).astype(jnp.int32)
    (mine,) = after([mine], before_own, rings, place)
    partner = step(mine, (0, 1), (1, 0), (2, 3), (3, 2))
    across = step(mine, (1, 2), (2, 1))
    early = both(mine)

    args = (rings, skip, queries, key_proj, value_proj)
    firsts = gate(*args, before_own, window, half)[::-1]
    crossed = [swapped(f, 2, devices) for f in firsts]
    before_theirs = swapped(*after([before_theirs], *firsts), 1, devices)
    theirs = gate(*args, before_theirs, 1 - window, half, [early[1]])[::-1]
    partner, across = after([partner, across], *theirs, crossed[0])
    handed = step(across, (1, 0), (2, 3))
    kept = step(partner, (1, 2), (2, 1))
    early += both(partner)
    seconds = [swapped(theirs[0], devices // 2, devices)]
    for t in theirs[1:]:
        seconds += [swapped(*after([t], crossed[0]), devices // 2, devices)]
    far = [swapped(*after([seconds[0]], crossed[-1]), 2, devices)]
    far += [swapped(swapped(o, 3, devices), 1, devices) for o in seconds[1:]]
    handed, kept = after([handed, kept], far[0], seconds[-1])
    final = step(kept, (1, 0), (2, 3))
    at_end = jnp.where((plane == 0) | (plane == planes - 1), 0, 1)
    gathered = list(zip(firsts, crossed, seconds, far))
    def sent_back(send):
        return swapped(send, devices // 2, devices)

    sums = []

    def summed(rows, weights):
        keep, send = project(rows, weights, [F32, BF16], [v for _, v, _ in sums[-1:]])
        sums.append((keep, send, sent_back(send)))

    single = [[w] for w in early]
    for pieces in gathered:
        summed(pieces, single)
    everyone = [gathered[blocks - 1 - b][p] for p in range(4) for b in range(blocks)]
    keep, send = project(everyone, list(zip(both(handed), both(across))), [F32, BF16], [sums[-1][1]], at_end)
    sums.append((keep, send, sent_back(send)))
    settled = [settle(k, arrived, [send] if i < blocks else []) for i, (k, _, arrived) in enumerate(sums)]
    parts = [[n, swapped(f, 2, devices)] for n, f in settled]

    kept = both(kept)
    final = both(*after([final], parts[0][1], settled[blocks - 1][0], send, kept[1]))
    keep, send = project(everyone, list(zip(final, kept)), [F32, BF16], [], at_end)
    total = None
    for i, block in enumerate(reversed(range(blocks))):
        total = add_slots(residual, total, [parts[i]], block, place, 0, 2)
    near, far_rows = settle(keep, sent_back(send), [total])
    last_part = [near, swapped(far_rows, 2, devices)]
    total = add_slots(residual, total, [parts[blocks]], 0, place, 2, 1, [near])
    return add_slots(residual, total, [last_part], 0, place, 3, 1)


def general(queries, key_proj, value_proj, filter_taps, skip_gain, out_weight, residual):
    seq_len, channels = queries.shape
    rows = filter_taps.shape[1]
    outgoing = product_of(key_proj[seq_len - rows :], value_proj[seq_len - rows :])
    count = lax.axis_size(SEQ)
    before = lax.ppermute(outgoing, SEQ, [(i, i + 1) for i in range(count - 1)])
    rings, skip = rings_of(filter_taps), skip_gain[None, :]
    gated = gate(rings, skip, queries, key_proj, value_proj, before, jnp.int32(0), channels)
    gated = jnp.concatenate(gated, axis=0)
    weight = lax.all_gather(out_weight, SEQ, axis=1, tiled=True)
    projected = jnp.dot(gated, weight, preferred_element_type=F32)
    share = lax.psum_scatter(projected, "chan", scatter_dimension=1, tiled=True)
    return (residual.astype(F32) + share).astype(BF16)


def solution(mesh):
    sizes = mesh.shape
    fits = sizes["groups"] == 2 and sizes["chan"] == 1 and sizes["section"] == 2 and sizes["seq"] % 2 == 0
    return jax.shard_map(
        paired if fits and sizes["seq"] == 8 else general,
        mesh=mesh,
        in_specs=(
            P(("groups", "seq", "section"), "chan"),
            P(("groups", "seq", "section"), "chan"),
            P(("groups", "seq", "section"), "chan"),
            P("chan", None),
            P("chan"),
            P("chan", ("seq", "section")),
            P(("groups", "seq", "section"), "chan"),
        ),
        out_specs=P(("groups", "seq", "section"), "chan"),
        check_vma=False,
    )
```

```python
import functools

import jax
import jax.numpy as jnp
from jax import lax
from jax.experimental import pallas as pl
from jax.experimental.pallas import tpu as pltpu
from jax.sharding import PartitionSpec as P

LANES = 128
SEQ = ("seq", "section")
EVERY = ("groups", "seq", "section")
F32, BF16 = jnp.float32, jnp.bfloat16


def cost(us):
    return pl.CostEstimate(flops=int(us * 1.1e9), bytes_accessed=1, transcendentals=0)


def pass_kernel(*refs):
    pass


def after(values, *waits, weight=0):
    return pl.pallas_call(
        pass_kernel,
        in_specs=[pl.BlockSpec(memory_space=pl.ANY)] * (len(values) + len(waits)),
        out_specs=[pl.BlockSpec(memory_space=pl.ANY)] * len(values),
        out_shape=[jax.ShapeDtypeStruct(v.shape, v.dtype) for v in values],
        input_output_aliases={i: i for i in range(len(values))},
        compiler_params=pltpu.CompilerParams(vmem_limit_bytes=16 << 20),
        cost_estimate=cost(weight),
    )(*values, *waits)


def product_of(key, value):
    return (key.astype(F32) * value.astype(F32)).astype(BF16)


def gate_kernel(per_group, blocks, start_ref, ring_ref, skip_ref, q_ref, k_ref, v_ref, before_ref, *rest):
    out_refs = rest[-blocks:]
    rows, width = out_refs[0].shape
    groups = LANES // per_group
    row = lax.broadcasted_iota(jnp.int32, (rows, rows), 0)
    col = lax.broadcasted_iota(jnp.int32, (rows, rows), 1)
    keep = (row >= col).astype(F32).astype(BF16)
    lane_group = lax.broadcasted_iota(jnp.int32, (2 * rows, blocks * LANES), 1) % LANES // per_group

    def step(t, carry):
        lanes = pl.ds(pl.multiple_of(t * LANES, LANES), LANES)
        spans = [slice(b * rows, (b + 1) * rows) for b in range(blocks)]
        products = [product_of(k_ref[span, lanes], v_ref[span, lanes]) for span in spans]
        before = [before_ref[:, lanes]] + products[:-1]
        data = jnp.concatenate([jnp.concatenate(products, axis=1), jnp.concatenate(before, axis=1)], axis=0)
        rings = ring_ref[pl.ds(pl.multiple_of(t * groups, groups), groups), :]
        left, right = [], []
        for g in range(groups):
            ring = jnp.broadcast_to(rings[g : g + 1, :], (rows, rows))
            ring = pltpu.roll(ring, 0, 1, stride=1, stride_axis=0).astype(BF16)
            lower = ring * keep
            left += [lower, ring - lower]
            right.append(jnp.where(lane_group == g, data, jnp.zeros_like(data)))
        convolved = jnp.dot(
            jnp.concatenate(left, axis=1), jnp.concatenate(right, axis=0), preferred_element_type=F32
        )
        skip = skip_ref[:, lanes]
        for b, span in enumerate(spans):
            here = convolved[:, b * LANES : (b + 1) * LANES] + skip * products[b].astype(F32)
            out_refs[b][:, lanes] = (q_ref[span, lanes].astype(F32) * here).astype(BF16)
        return carry

    lax.fori_loop(0, width // LANES, step, 0)


def gate(rings, skip, queries, key_proj, value_proj, before, start, count, waits=()):
    rows = rings.shape[1]
    seq_len, channels = queries.shape
    blocks = seq_len // rows
    per_group = channels // rings.shape[0]
    tile = min(512, count)
    steps = count // tile

    def at(height):
        return pl.BlockSpec((height, tile), lambda i, s: (0, s[0] * steps + i))

    return pl.pallas_call(
        functools.partial(gate_kernel, per_group, blocks),
        grid_spec=pltpu.PrefetchScalarGridSpec(
            num_scalar_prefetch=1,
            grid=(steps,),
            in_specs=[
                pl.BlockSpec((tile // per_group, rows), lambda i, s: (s[0] * steps + i, 0)),
                at(1),
                at(seq_len),
                at(seq_len),
                at(seq_len),
                pl.BlockSpec((rows, tile), lambda i, s: (0, i)),
            ]
            + [pl.BlockSpec(memory_space=pl.ANY)] * len(waits),
            out_specs=[pl.BlockSpec((rows, tile), lambda i, s: (0, i))] * blocks,
        ),
        out_shape=[jax.ShapeDtypeStruct((rows, count), BF16)] * blocks,
        compiler_params=pltpu.CompilerParams(vmem_limit_bytes=60 << 20),
        cost_estimate=cost(0.1),
    )(jnp.reshape(start, (1,)).astype(jnp.int32), rings, skip, queries, key_proj, value_proj, before, *waits)


def rings_of(filter_taps):
    return jnp.roll(filter_taps[:, ::-1], 1, axis=1).astype(F32)


def project_kernel(row_count, choices, weight_count, outs, which_ref, *refs):
    rows, weights = refs[:row_count], refs[row_count : row_count + choices * weight_count]
    out_refs, total = refs[-1 - outs : -1], refs[-1]
    step = pl.program_id(0)

    @pl.when(step == 0)
    def _():
        total[...] = jnp.zeros_like(total)

    left = jnp.concatenate([r[...] for r in rows], axis=0)
    for n in range(choices):

        @pl.when(which_ref[0] == n)
        def _():
            right = jnp.concatenate([w[...] for w in weights[n::choices]], axis=1)
            total[...] += jnp.dot(left, right, preferred_element_type=F32)

    @pl.when(step == pl.num_programs(0) - 1)
    def _():
        part = out_refs[0].shape[0]
        for i, out_ref in enumerate(out_refs):
            out_ref[...] = total[i * part : (i + 1) * part, :].astype(out_ref.dtype)


def project(rows, weights, dtypes, waits=(), which=0):
    depth = rows[0].shape[1]
    height = sum(r.shape[0] for r in rows)
    widths = [w[0].shape[1] for w in weights]
    tile = min(1024, depth)
    choices = len(weights[0])

    def weight_spec(width, n):
        if choices == 1:
            return pl.BlockSpec((tile, width), lambda k, s: (k, 0))
        return pl.BlockSpec((tile, width), lambda k, s: (jnp.where(s[0] == n, k, 0), 0))

    part = (height // len(dtypes), sum(widths))
    return pl.pallas_call(
        functools.partial(project_kernel, len(rows), choices, len(weights), len(dtypes)),
        grid_spec=pltpu.PrefetchScalarGridSpec(
            num_scalar_prefetch=1,
            grid=(depth // tile,),
            in_specs=[pl.BlockSpec((r.shape[0], tile), lambda k, s: (0, k)) for r in rows]
            + [weight_spec(width, n) for width in widths for n in range(choices)]
            + [pl.BlockSpec(memory_space=pl.ANY)] * len(waits),
            out_specs=[pl.BlockSpec(part, lambda k, s: (0, 0))] * len(dtypes),
            scratch_shapes=[pltpu.VMEM((height, sum(widths)), F32)],
        ),
        out_shape=[jax.ShapeDtypeStruct(part, dtype) for dtype in dtypes],
        compiler_params=pltpu.CompilerParams(vmem_limit_bytes=24 << 20),
        cost_estimate=cost(1),
    )(jnp.full((1,), which, jnp.int32), *rows, *[w for group in weights for w in group], *waits)


def settle_kernel(keep_ref, arrived_ref, *refs):
    near_ref, far_ref = refs[-2:]
    rows = near_ref.shape[0]
    near_ref[...] = (keep_ref[:rows, :] + arrived_ref[:rows, :].astype(F32)).astype(BF16)
    far_ref[...] = (keep_ref[rows:, :] + arrived_ref[rows:, :].astype(F32)).astype(BF16)


def settle(keep, arrived, waits=()):
    rows, width = keep.shape
    tile = min(512, width)
    whole = pl.BlockSpec((rows, tile), lambda i: (0, i))
    return pl.pallas_call(
        settle_kernel,
        grid=(width // tile,),
        in_specs=[whole, whole] + [pl.BlockSpec(memory_space=pl.ANY)] * len(waits),
        out_specs=[pl.BlockSpec((rows // 2, tile), lambda i: (0, i))] * 2,
        out_shape=[jax.ShapeDtypeStruct((rows // 2, width), BF16)] * 2,
        compiler_params=pltpu.CompilerParams(vmem_limit_bytes=16 << 20),
        cost_estimate=cost(0),
    )(keep, arrived, *waits)


def add_kernel(counts, place_ref, *refs):
    residual_ref, out_ref = refs[0], refs[-1]
    step, at, first = pl.program_id(0), 1, 0
    for slots, heights in counts:
        near, far = refs[at : at + len(heights)], refs[at + len(heights) : at + 2 * len(heights)]

        @pl.when((step >= first) & (step < first + slots))
        def _():
            top = 0
            for height, pair in zip(heights, zip(near, far)):
                rows, top = slice(top, top + height), top + height
                for j in range(4):
                    width = pair[0].shape[1] // 2
                    lanes = pl.ds(pl.multiple_of(place_ref[j] * width, LANES), width)
                    mine = pair[j // 2][:, (j % 2) * width : (j % 2 + 1) * width]
                    out_ref[rows, lanes] = (residual_ref[rows, lanes].astype(F32) + mine.astype(F32)).astype(BF16)

        at, first = at + 2 * len(heights), first + slots


def add_slots(residual, groups, place, start=0, total=None, waits=()):
    rows = residual.shape[0]
    span = groups[0][1][0].shape[1] // groups[0][0] * 2
    whole = pl.BlockSpec((rows, span), lambda i, s: (0, s[4 + start + i]))
    so_far = ([] if total is None else [total]) + list(waits)
    specs, operands, counts, first = [], [], [], 0
    for slots, near, far in groups:
        for piece in [*near, *far]:

            def at(i, s, first=first, slots=slots):
                return (0, jnp.clip(i - first, 0, slots - 1))

            specs.append(pl.BlockSpec((piece.shape[0], span // 2), at))
            operands.append(piece)
        counts.append((slots, [n.shape[0] for n in near]))
        first += slots
    return pl.pallas_call(
        functools.partial(add_kernel, counts),
        grid_spec=pltpu.PrefetchScalarGridSpec(
            num_scalar_prefetch=1,
            grid=(first,),
            in_specs=[whole] + specs + [pl.BlockSpec(memory_space=pl.ANY)] * len(so_far),
            out_specs=whole,
        ),
        out_shape=jax.ShapeDtypeStruct(residual.shape, residual.dtype),
        input_output_aliases={} if total is None else {2 + len(operands): 0},
        compiler_params=pltpu.CompilerParams(vmem_limit_bytes=16 << 20),
        cost_estimate=cost(1),
    )(place, residual, *operands, *so_far)


def finish_kernel(place_ref, *refs):
    residual_ref, out_ref = refs[0], refs[-1]
    width = refs[1].shape[1]
    for j in range(4):
        lanes = pl.ds(pl.multiple_of(place_ref[j] * width, LANES), width)
        out_ref[:, lanes] = (residual_ref[:, lanes].astype(F32) + refs[1 + j][...].astype(F32)).astype(BF16)


def finish(residual, total, terms, place, slot):
    rows, width = terms[0].shape
    whole = pl.BlockSpec((rows, 4 * width), lambda i, s: (0, s[4 + slot]))
    return pl.pallas_call(
        finish_kernel,
        grid_spec=pltpu.PrefetchScalarGridSpec(
            num_scalar_prefetch=1,
            grid=(1,),
            in_specs=[whole]
            + [pl.BlockSpec((rows, width), lambda i, s: (0, 0))] * len(terms)
            + [pl.BlockSpec(memory_space=pl.ANY)],
            out_specs=whole,
        ),
        out_shape=jax.ShapeDtypeStruct(residual.shape, residual.dtype),
        input_output_aliases={2 + len(terms): 0},
        compiler_params=pltpu.CompilerParams(vmem_limit_bytes=16 << 20),
        cost_estimate=cost(1),
    )(place, residual, *terms, total)


def swapped(value, bit, devices):
    return lax.ppermute(value, EVERY, [(d, d ^ bit) for d in range(devices)])


def paired(queries, key_proj, value_proj, filter_taps, skip_gain, out_weight, residual):
    seq_len, channels = queries.shape
    rows = filter_taps.shape[1]
    blocks = seq_len // rows
    half = channels // 2
    devices = 2 * lax.axis_size("seq") * 2
    window, section = lax.axis_index("groups"), lax.axis_index("section")
    planes = lax.axis_size("seq") // 2
    plane, side = lax.axis_index("seq") // 2, lax.axis_index("seq") % 2

    last = seq_len - rows
    shards = planes * 4
    edge = [(w * shards + i, w * shards + i + 1) for w in range(2) for i in range(shards - 1)]

    def outgoing(start, spare):
        product = product_of(
            lax.dynamic_slice(key_proj, (last, start), (rows, half)),
            lax.dynamic_slice(value_proj, (last, start), (rows, half)),
        )
        return jnp.pad(product, ((0, spare), (0, 0)))

    before_own = lax.ppermute(outgoing(window * half, 0), EVERY, edge)
    before_theirs = lax.ppermute(outgoing((1 - window) * half, 16), EVERY, [(p, q ^ 1) for p, q in edge])

    def step(value, *pairs):
        return lax.ppermute(
            value, EVERY, [(w * shards + p * 4 + i, w * shards + q * 4 + i) for w in range(2) for p, q in pairs for i in range(4)]
        )

    def both(value):
        return [value, swapped(value, 1, devices)]

    mine = lax.dynamic_slice_in_dim(out_weight, window * half, half, 0)
    rings, skip = rings_of(filter_taps), skip_gain[None, :]
    order = [side * 2 + section, side * 2 + 1 - section, 2 - side * 2 + section, 3 - side * 2 - section]
    slots = [[0, 1, 2, 3], [1, 0, 3, 2], [2, 2, 1, 1], [3, 3, 0, 0]]
    held = [sum(jnp.where(plane == z, p, 0) for z, p in enumerate(slot)) for slot in slots]
    place = jnp.stack(order + held).astype(jnp.int32)
    (mine,) = after([mine], before_own, rings, place)
    partner = step(mine, (0, 1), (1, 0), (2, 3), (3, 2))
    across = step(mine, (1, 2), (2, 1))
    early = both(mine)

    args = (rings, skip, queries, key_proj, value_proj)
    firsts = gate(*args, before_own, window, half)[::-1]
    crossed = [swapped(f, 2, devices) for f in firsts]
    before_theirs = swapped(*after([before_theirs], *firsts), 1, devices)
    theirs = gate(*args, before_theirs, 1 - window, half, [early[1]])[::-1]
    partner, across = after([partner, across], *theirs, crossed[0])
    handed = step(across, (1, 0), (2, 3))
    kept = step(partner, (1, 2), (2, 1))
    early += both(partner)
    seconds = [swapped(theirs[0], devices // 2, devices)]
    for t in theirs[1:]:
        seconds += [swapped(*after([t], crossed[0]), devices // 2, devices)]
    far = [swapped(*after([seconds[0]], crossed[-1]), 2, devices)]
    far += [swapped(o, 3, devices) for o in seconds[1:]]
    handed, kept = after([handed, kept], far[0], seconds[-1])
    final = step(kept, (1, 0), (2, 3))
    at_end = jnp.where((plane == 0) | (plane == planes - 1), 0, 1)
    def sent_back(send):
        return swapped(send, devices // 2, devices)

    sums = []

    def summed(rows, weights):
        keep, send = project(rows, weights, [F32, BF16], [v for _, v, _ in sums[-1:]])
        sums.append((keep, send, sent_back(send)))

    single = [[w] for w in early]
    gathered = []
    for n, pieces in enumerate(zip(firsts, crossed, seconds, far)):
        if n:
            pieces = [*pieces[:3], swapped(*after([pieces[3]], sums[-1][1]), 1, devices)]
        gathered.append(pieces)
        summed(pieces, single)
    everyone = [gathered[blocks - 1 - b][p] for p in range(4) for b in range(blocks)]
    keep, send = project(everyone, list(zip(both(handed), both(across))), [F32, BF16], [sums[-1][1]], at_end)
    sums.append((keep, send, sent_back(send)))
    settled = [settle(k, arrived, [sums[i + 1][1]] if i < blocks else []) for i, (k, _, arrived) in enumerate(sums)]
    parts = [[n, swapped(f, 2, devices)] for n, f in settled]

    kept = both(kept)
    (final,) = after([final], *[p[1] for p in parts[: blocks - 1]], settled[blocks - 1][0], sums[blocks][2], kept[1])
    final = both(final)
    waits, last = [], []
    for n in range(2):
        keep, send = project(everyone, [(final[n], kept[n])], [F32, BF16], waits, at_end)
        waits = [send, parts[blocks - 1][1]]
        last.append((keep, sent_back(send)))
    near, far_rows = settle(*last[0])
    terms = [[near, swapped(far_rows, 2, devices)]]
    near, far_rows = settle(*last[1], [terms[0][1], parts[blocks][1]])
    terms.append([near, swapped(far_rows, 2, devices)])
    rows_up = parts[:blocks][::-1]
    groups = [(2, [p[0] for p in rows_up], [p[1] for p in rows_up]), (1, [parts[blocks][0]], [parts[blocks][1]])]
    total = add_slots(residual, groups, place, waits=[near])
    return finish(residual, total, [terms[dc][dx] for dx in range(2) for dc in range(2)], place, 3)


def general(queries, key_proj, value_proj, filter_taps, skip_gain, out_weight, residual):
    seq_len, channels = queries.shape
    rows = filter_taps.shape[1]
    outgoing = product_of(key_proj[seq_len - rows :], value_proj[seq_len - rows :])
    count = lax.axis_size(SEQ)
    before = lax.ppermute(outgoing, SEQ, [(i, i + 1) for i in range(count - 1)])
    rings, skip = rings_of(filter_taps), skip_gain[None, :]
    gated = gate(rings, skip, queries, key_proj, value_proj, before, jnp.int32(0), channels)
    gated = jnp.concatenate(gated, axis=0)
    weight = lax.all_gather(out_weight, SEQ, axis=1, tiled=True)
    projected = jnp.dot(gated, weight, preferred_element_type=F32)
    share = lax.psum_scatter(projected, "chan", scatter_dimension=1, tiled=True)
    return (residual.astype(F32) + share).astype(BF16)


def solution(mesh):
    sizes = mesh.shape
    fits = sizes["groups"] == 2 and sizes["chan"] == 1 and sizes["section"] == 2 and sizes["seq"] % 2 == 0
    return jax.shard_map(
        paired if fits and sizes["seq"] == 8 else general,
        mesh=mesh,
        in_specs=(
            P(("groups", "seq", "section"), "chan"),
            P(("groups", "seq", "section"), "chan"),
            P(("groups", "seq", "section"), "chan"),
            P("chan", None),
            P("chan"),
            P("chan", ("seq", "section")),
            P(("groups", "seq", "section"), "chan"),
        ),
        out_specs=P(("groups", "seq", "section"), "chan"),
        check_vma=False,
    )
```

```python
import functools

import jax
import jax.numpy as jnp
from jax import lax
from jax.experimental import pallas as pl
from jax.experimental.pallas import tpu as pltpu
from jax.sharding import PartitionSpec as P

LANES = 128
SEQ = ("seq", "section")
EVERY = ("groups", "seq", "section")
F32, BF16 = jnp.float32, jnp.bfloat16


def cost(us):
    return pl.CostEstimate(flops=int(us * 1.1e9), bytes_accessed=1, transcendentals=0)


def pass_kernel(*refs):
    pass


def after(values, *waits, weight=0, room=60):
    return pl.pallas_call(
        pass_kernel,
        in_specs=[pl.BlockSpec(memory_space=pl.ANY)] * (len(values) + len(waits)),
        out_specs=[pl.BlockSpec(memory_space=pl.ANY)] * len(values),
        out_shape=[jax.ShapeDtypeStruct(v.shape, v.dtype) for v in values],
        input_output_aliases={i: i for i in range(len(values))},
        compiler_params=pltpu.CompilerParams(vmem_limit_bytes=room << 20),
        cost_estimate=cost(weight),
    )(*values, *waits)


def product_of(key, value):
    return (key.astype(F32) * value.astype(F32)).astype(BF16)


def gate_kernel(per_group, blocks, start_ref, ring_ref, skip_ref, q_ref, k_ref, v_ref, before_ref, *rest):
    out_refs = rest[-blocks:]
    rows, width = out_refs[0].shape
    groups = LANES // per_group
    row = lax.broadcasted_iota(jnp.int32, (rows, rows), 0)
    col = lax.broadcasted_iota(jnp.int32, (rows, rows), 1)
    keep = (row >= col).astype(F32).astype(BF16)
    lane_group = lax.broadcasted_iota(jnp.int32, (2 * rows, blocks * LANES), 1) % LANES // per_group

    def step(t, carry):
        lanes = pl.ds(pl.multiple_of(t * LANES, LANES), LANES)
        spans = [slice(b * rows, (b + 1) * rows) for b in range(blocks)]
        products = [product_of(k_ref[span, lanes], v_ref[span, lanes]) for span in spans]
        before = [before_ref[:, lanes]] + products[:-1]
        data = jnp.concatenate([jnp.concatenate(products, axis=1), jnp.concatenate(before, axis=1)], axis=0)
        rings = ring_ref[pl.ds(pl.multiple_of(t * groups, groups), groups), :]
        left, right = [], []
        for g in range(groups):
            ring = jnp.broadcast_to(rings[g : g + 1, :], (rows, rows))
            ring = pltpu.roll(ring, 0, 1, stride=1, stride_axis=0).astype(BF16)
            lower = ring * keep
            left += [lower, ring - lower]
            right.append(jnp.where(lane_group == g, data, jnp.zeros_like(data)))
        convolved = jnp.dot(
            jnp.concatenate(left, axis=1), jnp.concatenate(right, axis=0), preferred_element_type=F32
        )
        skip = skip_ref[:, lanes]
        for b, span in enumerate(spans):
            here = convolved[:, b * LANES : (b + 1) * LANES] + skip * products[b].astype(F32)
            out_refs[b][:, lanes] = (q_ref[span, lanes].astype(F32) * here).astype(BF16)
        return carry

    lax.fori_loop(0, width // LANES, step, 0)


def gate(rings, skip, queries, key_proj, value_proj, before, start, count, waits=()):
    rows = rings.shape[1]
    seq_len, channels = queries.shape
    blocks = seq_len // rows
    per_group = channels // rings.shape[0]
    tile = min(512, count)
    steps = count // tile

    def at(height):
        return pl.BlockSpec((height, tile), lambda i, s: (0, s[0] * steps + i))

    return pl.pallas_call(
        functools.partial(gate_kernel, per_group, blocks),
        grid_spec=pltpu.PrefetchScalarGridSpec(
            num_scalar_prefetch=1,
            grid=(steps,),
            in_specs=[
                pl.BlockSpec((tile // per_group, rows), lambda i, s: (s[0] * steps + i, 0)),
                at(1),
                at(seq_len),
                at(seq_len),
                at(seq_len),
                pl.BlockSpec((rows, tile), lambda i, s: (0, i)),
            ]
            + [pl.BlockSpec(memory_space=pl.ANY)] * len(waits),
            out_specs=[pl.BlockSpec((rows, tile), lambda i, s: (0, i))] * blocks,
        ),
        out_shape=[jax.ShapeDtypeStruct((rows, count), BF16)] * blocks,
        compiler_params=pltpu.CompilerParams(vmem_limit_bytes=60 << 20),
        cost_estimate=cost(0.1),
    )(jnp.reshape(start, (1,)).astype(jnp.int32), rings, skip, queries, key_proj, value_proj, before, *waits)


def rings_of(filter_taps):
    return jnp.roll(filter_taps[:, ::-1], 1, axis=1).astype(F32)


def project_kernel(row_count, choices, weight_count, outs, which_ref, *refs):
    rows, weights = refs[:row_count], refs[row_count : row_count + choices * weight_count]
    out_refs, total = refs[-1 - outs : -1], refs[-1]
    step = pl.program_id(0)

    @pl.when(step == 0)
    def _():
        total[...] = jnp.zeros_like(total)

    left = jnp.concatenate([r[...] for r in rows], axis=0)
    for n in range(choices):

        @pl.when(which_ref[0] == n)
        def _():
            right = jnp.concatenate([w[...] for w in weights[n::choices]], axis=1)
            total[...] += jnp.dot(left, right, preferred_element_type=F32)

    @pl.when(step == pl.num_programs(0) - 1)
    def _():
        part = out_refs[0].shape[0]
        for i, out_ref in enumerate(out_refs):
            out_ref[...] = total[i * part : (i + 1) * part, :].astype(out_ref.dtype)


def project(rows, weights, dtypes, waits=(), which=0, room=60):
    depth = rows[0].shape[1]
    height = sum(r.shape[0] for r in rows)
    widths = [w[0].shape[1] for w in weights]
    tile = min(1024, depth)
    choices = len(weights[0])

    def weight_spec(width, n):
        if choices == 1:
            return pl.BlockSpec((tile, width), lambda k, s: (k, 0))
        return pl.BlockSpec((tile, width), lambda k, s: (jnp.where(s[0] == n, k, 0), 0))

    part = (height // len(dtypes), sum(widths))
    return pl.pallas_call(
        functools.partial(project_kernel, len(rows), choices, len(weights), len(dtypes)),
        grid_spec=pltpu.PrefetchScalarGridSpec(
            num_scalar_prefetch=1,
            grid=(depth // tile,),
            in_specs=[pl.BlockSpec((r.shape[0], tile), lambda k, s: (0, k)) for r in rows]
            + [weight_spec(width, n) for width in widths for n in range(choices)]
            + [pl.BlockSpec(memory_space=pl.ANY)] * len(waits),
            out_specs=[pl.BlockSpec(part, lambda k, s: (0, 0))] * len(dtypes),
            scratch_shapes=[pltpu.VMEM((height, sum(widths)), F32)],
        ),
        out_shape=[jax.ShapeDtypeStruct(part, dtype) for dtype in dtypes],
        compiler_params=pltpu.CompilerParams(vmem_limit_bytes=room << 20),
        cost_estimate=cost(1),
    )(jnp.full((1,), which, jnp.int32), *rows, *[w for group in weights for w in group], *waits)


def settle_kernel(keep_ref, arrived_ref, *refs):
    near_ref, far_ref = refs[-2:]
    rows = near_ref.shape[0]
    near_ref[...] = (keep_ref[:rows, :] + arrived_ref[:rows, :].astype(F32)).astype(BF16)
    far_ref[...] = (keep_ref[rows:, :] + arrived_ref[rows:, :].astype(F32)).astype(BF16)


def settle(keep, arrived, waits=()):
    rows, width = keep.shape
    tile = min(512, width)
    whole = pl.BlockSpec((rows, tile), lambda i: (0, i))
    return pl.pallas_call(
        settle_kernel,
        grid=(width // tile,),
        in_specs=[whole, whole] + [pl.BlockSpec(memory_space=pl.ANY)] * len(waits),
        out_specs=[pl.BlockSpec((rows // 2, tile), lambda i: (0, i))] * 2,
        out_shape=[jax.ShapeDtypeStruct((rows // 2, width), BF16)] * 2,
        compiler_params=pltpu.CompilerParams(vmem_limit_bytes=16 << 20),
        cost_estimate=cost(0),
    )(keep, arrived, *waits)


def add_kernel(counts, place_ref, *refs):
    residual_ref, out_ref = refs[0], refs[-1]
    step, at, first = pl.program_id(0), 1, 0
    for slots, heights in counts:
        near, far = refs[at : at + len(heights)], refs[at + len(heights) : at + 2 * len(heights)]

        @pl.when((step >= first) & (step < first + slots))
        def _():
            top = 0
            for height, pair in zip(heights, zip(near, far)):
                rows, top = slice(top, top + height), top + height
                for j in range(4):
                    width = pair[0].shape[1] // 2
                    lanes = pl.ds(pl.multiple_of(place_ref[j] * width, LANES), width)
                    mine = pair[j // 2][:, (j % 2) * width : (j % 2 + 1) * width]
                    out_ref[rows, lanes] = (residual_ref[rows, lanes].astype(F32) + mine.astype(F32)).astype(BF16)

        at, first = at + 2 * len(heights), first + slots


def add_slots(residual, groups, place, start=0, total=None, waits=()):
    rows = residual.shape[0]
    span = groups[0][1][0].shape[1] // groups[0][0] * 2
    whole = pl.BlockSpec((rows, span), lambda i, s: (0, s[4 + start + i]))
    so_far = ([] if total is None else [total]) + list(waits)
    specs, operands, counts, first = [], [], [], 0
    for slots, near, far in groups:
        for piece in [*near, *far]:

            def at(i, s, first=first, slots=slots):
                return (0, jnp.clip(i - first, 0, slots - 1))

            specs.append(pl.BlockSpec((piece.shape[0], span // 2), at))
            operands.append(piece)
        counts.append((slots, [n.shape[0] for n in near]))
        first += slots
    return pl.pallas_call(
        functools.partial(add_kernel, counts),
        grid_spec=pltpu.PrefetchScalarGridSpec(
            num_scalar_prefetch=1,
            grid=(first,),
            in_specs=[whole] + specs + [pl.BlockSpec(memory_space=pl.ANY)] * len(so_far),
            out_specs=whole,
        ),
        out_shape=jax.ShapeDtypeStruct(residual.shape, residual.dtype),
        input_output_aliases={} if total is None else {2 + len(operands): 0},
        compiler_params=pltpu.CompilerParams(vmem_limit_bytes=16 << 20),
        cost_estimate=cost(1),
    )(place, residual, *operands, *so_far)


def finish_kernel(place_ref, *refs):
    residual_ref, out_ref = refs[0], refs[-1]
    width = refs[1].shape[1]
    for j in range(4):
        lanes = pl.ds(pl.multiple_of(place_ref[j] * width, LANES), width)
        out_ref[:, lanes] = (residual_ref[:, lanes].astype(F32) + refs[1 + j][...].astype(F32)).astype(BF16)


def finish(residual, total, terms, place, slot):
    rows, width = terms[0].shape
    whole = pl.BlockSpec((rows, 4 * width), lambda i, s: (0, s[4 + slot]))
    return pl.pallas_call(
        finish_kernel,
        grid_spec=pltpu.PrefetchScalarGridSpec(
            num_scalar_prefetch=1,
            grid=(1,),
            in_specs=[whole]
            + [pl.BlockSpec((rows, width), lambda i, s: (0, 0))] * len(terms)
            + [pl.BlockSpec(memory_space=pl.ANY)],
            out_specs=whole,
        ),
        out_shape=jax.ShapeDtypeStruct(residual.shape, residual.dtype),
        input_output_aliases={2 + len(terms): 0},
        compiler_params=pltpu.CompilerParams(vmem_limit_bytes=16 << 20),
        cost_estimate=cost(1),
    )(place, residual, *terms, total)


def swapped(value, bit, devices):
    return lax.ppermute(value, EVERY, [(d, d ^ bit) for d in range(devices)])


def paired(queries, key_proj, value_proj, filter_taps, skip_gain, out_weight, residual):
    seq_len, channels = queries.shape
    rows = filter_taps.shape[1]
    blocks = seq_len // rows
    half = channels // 2
    devices = 2 * lax.axis_size("seq") * 2
    window, section = lax.axis_index("groups"), lax.axis_index("section")
    planes = lax.axis_size("seq") // 2
    plane, side = lax.axis_index("seq") // 2, lax.axis_index("seq") % 2

    last = seq_len - rows
    shards = planes * 4
    edge = [(w * shards + i, w * shards + i + 1) for w in range(2) for i in range(shards - 1)]

    def outgoing(start, spare):
        product = product_of(
            lax.dynamic_slice(key_proj, (last, start), (rows, half)),
            lax.dynamic_slice(value_proj, (last, start), (rows, half)),
        )
        return jnp.pad(product, ((0, spare), (0, 0)))

    before_own = lax.ppermute(outgoing(window * half, 0), EVERY, edge)
    before_theirs = lax.ppermute(outgoing((1 - window) * half, 16), EVERY, [(p, q ^ 1) for p, q in edge])

    def step(value, *pairs):
        return lax.ppermute(
            value, EVERY, [(w * shards + p * 4 + i, w * shards + q * 4 + i) for w in range(2) for p, q in pairs for i in range(4)]
        )

    def both(value):
        return [value, swapped(value, 1, devices)]

    mine = lax.dynamic_slice_in_dim(out_weight, window * half, half, 0)
    rings, skip = rings_of(filter_taps), skip_gain[None, :]
    order = [side * 2 + section, side * 2 + 1 - section, 2 - side * 2 + section, 3 - side * 2 - section]
    slots = [[0, 1, 2, 3], [1, 0, 3, 2], [2, 2, 1, 1], [3, 3, 0, 0]]
    held = [sum(jnp.where(plane == z, p, 0) for z, p in enumerate(slot)) for slot in slots]
    place = jnp.stack(order + held).astype(jnp.int32)
    (mine,) = after([mine], before_own, rings, place)
    partner = step(mine, (0, 1), (1, 0), (2, 3), (3, 2))
    across = step(mine, (1, 2), (2, 1))
    early = both(mine)

    args = (rings, skip, queries, key_proj, value_proj)
    firsts = gate(*args, before_own, window, half)[::-1]
    crossed = [swapped(f, 2, devices) for f in firsts]
    before_theirs = swapped(*after([before_theirs], *firsts), 1, devices)
    theirs = gate(*args, before_theirs, 1 - window, half, [early[1]])[::-1]
    partner, across = after([partner, across], *theirs, crossed[0])
    handed = step(across, (1, 0), (2, 3))
    kept = step(partner, (1, 2), (2, 1))
    early += both(partner)
    seconds = [swapped(theirs[0], devices // 2, devices)]
    for t in theirs[1:]:
        seconds += [swapped(*after([t], crossed[0]), devices // 2, devices)]
    far = [swapped(*after([seconds[0]], crossed[-1]), 2, devices)]
    far += [swapped(o, 3, devices) for o in seconds[1:]]
    handed, kept = after([handed, kept], far[0], seconds[-1])
    final = step(kept, (1, 0), (2, 3))
    at_end = jnp.where((plane == 0) | (plane == planes - 1), 0, 1)
    def sent_back(send):
        return swapped(send, devices // 2, devices)

    sums = []

    def summed(rows, weights):
        keep, send = project(rows, weights, [F32, BF16], [v for _, v, _ in sums[-1:]])
        sums.append((keep, send, sent_back(send)))

    single = [[w] for w in early]
    gathered = []
    for n, pieces in enumerate(zip(firsts, crossed, seconds, far)):
        if n:
            pieces = [*pieces[:3], swapped(*after([pieces[3]], sums[-1][1]), 1, devices)]
        gathered.append(pieces)
        summed(pieces, single)
    everyone = [gathered[blocks - 1 - b][p] for p in range(4) for b in range(blocks)]
    keep, send = project(everyone, list(zip(both(handed), both(across))), [F32, BF16], [sums[-1][1]], at_end)
    sums.append((keep, send, sent_back(send)))
    settled = [settle(k, arrived, [sums[i + 1][1]] if i < blocks else []) for i, (k, _, arrived) in enumerate(sums)]
    parts = [[n, swapped(f, 2, devices)] for n, f in settled]

    kept = both(kept)
    (final,) = after([final], *[p[1] for p in parts[: blocks - 1]], settled[blocks - 1][0], sums[blocks][2], kept[1], room=16)
    final = both(final)
    waits, last = [], []
    for n in range(2):
        keep, send = project(everyone, [(final[n], kept[n])], [F32, BF16], waits, at_end, 24)
        waits = [send, parts[blocks - 1][1]]
        last.append((keep, sent_back(send)))
    near, far_rows = settle(*last[0])
    terms = [[near, swapped(far_rows, 2, devices)]]
    near, far_rows = settle(*last[1], [terms[0][1], parts[blocks][1]])
    terms.append([near, swapped(far_rows, 2, devices)])
    rows_up = parts[:blocks][::-1]
    groups = [(2, [p[0] for p in rows_up], [p[1] for p in rows_up]), (1, [parts[blocks][0]], [parts[blocks][1]])]
    total = add_slots(residual, groups, place, waits=[near])
    return finish(residual, total, [terms[dc][dx] for dx in range(2) for dc in range(2)], place, 3)


def general(queries, key_proj, value_proj, filter_taps, skip_gain, out_weight, residual):
    seq_len, channels = queries.shape
    rows = filter_taps.shape[1]
    outgoing = product_of(key_proj[seq_len - rows :], value_proj[seq_len - rows :])
    count = lax.axis_size(SEQ)
    before = lax.ppermute(outgoing, SEQ, [(i, i + 1) for i in range(count - 1)])
    rings, skip = rings_of(filter_taps), skip_gain[None, :]
    gated = gate(rings, skip, queries, key_proj, value_proj, before, jnp.int32(0), channels)
    gated = jnp.concatenate(gated, axis=0)
    weight = lax.all_gather(out_weight, SEQ, axis=1, tiled=True)
    projected = jnp.dot(gated, weight, preferred_element_type=F32)
    share = lax.psum_scatter(projected, "chan", scatter_dimension=1, tiled=True)
    return (residual.astype(F32) + share).astype(BF16)


def solution(mesh):
    sizes = mesh.shape
    fits = sizes["groups"] == 2 and sizes["chan"] == 1 and sizes["section"] == 2 and sizes["seq"] % 2 == 0
    return jax.shard_map(
        paired if fits and sizes["seq"] == 8 else general,
        mesh=mesh,
        in_specs=(
            P(("groups", "seq", "section"), "chan"),
            P(("groups", "seq", "section"), "chan"),
            P(("groups", "seq", "section"), "chan"),
            P("chan", None),
            P("chan"),
            P("chan", ("seq", "section")),
            P(("groups", "seq", "section"), "chan"),
        ),
        out_specs=P(("groups", "seq", "section"), "chan"),
        check_vma=False,
    )
```
